32 devices in a mesh: group: 2 (over y), batch: 8 (over z, x), tensor: 2 (over core).
Axes of the slice: x: 2, y: 2, z: 4, core: 2. Of those that a mesh axis runs over, the one named last changes fastest.
Arguments:
- hidden: bfloat16 [2, 2048, 8192], P(None, ('group', 'batch'), 'tensor'), parts along dimension 1, may hold values from -6 to 6
- value_projection_weight: bfloat16 [8192, 128], P('tensor'), may hold values from -0.0625 to 0.0625
- adapter_down_weight: bfloat16 [16, 8192, 64], P(('group', 'batch'), 'tensor'), parts along dimension 0, may hold values from -0.0625 to 0.0625
- adapter_up_weight: bfloat16 [16, 64, 128], P(('group', 'batch')), parts along dimension 0, may hold values from -0.75 to 0.75
- key_value_cache: bfloat16 [2048, 8, 256], P(('group', 'batch'), 'tensor'), parts along dimension 0, may hold values from -250 to 250
- query: bfloat16 [2, 2048, 1024], P(None, ('group', 'batch')), parts along dimension 1, may hold values from -6 to 6
- fresh_token_keys: bfloat16 [2, 2048, 128], P(None, ('group', 'batch')), parts along dimension 1, may hold values from -6 to 6
- adapter_per_row: int32 [2048, 1], P(('group', 'batch')), parts along dimension 0, may hold values from 0 to 7; in each aligned block of 128 rows (0 to 127, 128 to 255, ...) at most 16 rows name the same one
- cache_length: int32 [2048], P(('group', 'batch')), parts along dimension 0, may hold values from 1 to 8
- adapter_storage_index: int32 [16], P('group'), parts along dimension 0, may hold values from 0 to 7, each once
Outputs:
- context: bfloat16 [2, 2048, 1024], P(None, ('group', 'batch')), parts along dimension 1
The draws below stay inside these ranges and needn't reach their ends.
There are 2 independent parts, one for each index of `group`. The reference program is written for one: setup_inputs(seed, part) draws one part's arguments, and reference() takes and returns one part's arrays. A program takes and returns all parts, laid end to end along the dimension named above; an argument that names none is the same for every part. Nothing has to cross between parts.
Inputs may be any that keep to these rules, and one draw needn't show every extreme that they name: `adapter_per_row`: in each aligned block of 128 rows (the rows of one device) no adapter is named by more than 16 rows, a bound that some block reaches. `adapter_storage_index`: each storage position holds exactly one adapter.
All inputs are finite; a program needn't handle non-finite values.
Results may differ from the reference program's by a relative error of at most 0.012.
Values may be sent and summed in bfloat16 or wider, within the bound.
A program may use at most 64 MiB of HBM per device.

```python
import math
import jax
import jax.numpy as jnp
import numpy as np
from jax import lax

MODEL_WIDTH = 8192
HEAD_SIZE = 128
HQ = 8
ADAPTER_RANK = 64
ROW_DEV = 128
LEN = 8
ROWS = 1024
ADAPTER_COUNT = 8
CAP = 16
N_BATCH = 8


def draw_key_value_cache(key, part):
    key = jax.random.fold_in(key, 11)
    base_key = jax.random.fold_in(key, 0)
    cache = jnp.clip(jax.random.normal(base_key, (ROWS, LEN, 2 * HEAD_SIZE)), -5.0, 5.0)
    return cache.astype(jnp.bfloat16)


def with_ends(entries, rng, smallest, top_value):
    index_at = [jax.random.randint(jax.random.fold_in(rng, axis), (), 0, length) for axis, length in enumerate(entries.shape)]
    main_axis = entries.shape.index(max(entries.shape))
    beside = index_at[:main_axis] + [(index_at[main_axis] + 1) % entries.shape[main_axis]] + index_at[main_axis + 1:]
    return entries.at[tuple(index_at)].set(smallest).at[tuple(beside)].set(top_value)


def levels(rng, shape, shards, low, high):
    gain, own = 1.0, jax.random.fold_in(rng, 6)
    for axis_at, parts in shards:
        draws = jnp.exp(jax.random.uniform(jax.random.fold_in(own, axis_at), (parts,), jnp.float32, low / len(shards), high / len(shards)))
        gain = gain * jnp.repeat(draws, shape[axis_at] // parts).reshape([-1 if axis == axis_at else 1 for axis in range(len(shape))])
    return gain


def assign_block(stream_key, own, number, rows, number_of, top, limit, slope):
    order = jax.random.permutation(stream_key, number_of)
    crowded, usual = load_shares(number_of, rows * top, limit, slope, True), load_shares(number_of, rows * top, limit, slope, False)
    places = jnp.arange(number_of)

    def named(tallies, turn):
        used = int((tallies > 0).sum())
        fixed = max(1, used // 4)
        shifted = fixed + (places - fixed + turn * (used - fixed)) % max(1, number_of - fixed)
        return jnp.zeros((number_of,), jnp.int32).at[order[jnp.where(places < fixed, places, shifted)]].set(jnp.asarray(tallies, jnp.int32))

    tallies = jnp.where(number % 4 == 0, named(crowded, number // 4), named(usual, number - number // 4 - 1))
    mixed = jax.random.permutation(jax.random.fold_in(own, 3), number_of)
    source_of, taker = mixed[0:number_of // 2 * 2:2], mixed[1:number_of // 2 * 2:2]
    margin = jnp.minimum(tallies[source_of] - 1, limit - tallies[taker]) // 2
    margin = jnp.where((source_of == order[0]) | (taker == order[0]) | (tallies[taker] == 0), 0, jnp.maximum(margin, 0))
    shifted = jax.random.randint(jax.random.fold_in(own, 4), (number_of // 2,), 0, 1 << 20) % (margin + 1)
    tallies = tallies.at[source_of].add(-shifted).at[taker].add(shifted)
    items = jnp.searchsorted(jnp.cumsum(tallies), jnp.arange(rows * top), side="right").astype(jnp.int32)
    table = items.reshape(top, rows).T
    table = table[jax.random.permutation(jax.random.fold_in(own, 1), rows)]
    turn = jax.random.randint(jax.random.fold_in(own, 2), (rows, 1), 0, top)
    return jnp.take_along_axis(table, (jnp.arange(top)[None, :] + turn) % top, axis=1)


def load_shares(count, total, limit, slope, full):
    loads = [(1 << 20) // math.isqrt(standing ** slope) + 1 for standing in range(1, count + 1)]
    largest = limit if full else min(limit, max(-(-total // count), total * loads[0] // sum(loads)))
    least = 1 if total - largest >= count - 1 else 0
    holding, spare = [largest] + [least] * (count - 1), total - largest - least * (count - 1)
    while spare > 0:
        candidates = [i for i in range(1, count) if holding[i] < largest] or [i for i in range(1, count) if holding[i] < limit]
        whole, remaining = sum([loads[i] for i in candidates]), spare
        for i in candidates:
            more = min(limit - holding[i], max(1, remaining * loads[i] // whole), spare)
            holding[i] = holding[i] + more
            spare = spare - more
    return np.array(holding)


def centred(key, dims, spread, reach, cuts=(), held_as=jnp.bfloat16):
    level = levels(key, dims, cuts, -0.22, 0.18) if cuts else 1.0
    values = jax.random.normal(key, dims, jnp.float32) * spread * level
    return jnp.minimum(jnp.maximum(values, -reach), reach).astype(held_as)


def setup_inputs(seed: int = 0, part: int = 0) -> dict:
    seeds = jax.random.split(jax.random.key(seed), 11)
    part_keys = jax.random.split(jax.random.fold_in(seeds[10], part), 11)
    hidden = centred(part_keys[0], (2, ROWS, MODEL_WIDTH), 1.0, 6.0, ((1, 8), (2, 2)))
    value_projection_weight = centred(seeds[1], (MODEL_WIDTH, HEAD_SIZE), MODEL_WIDTH ** -0.5, 0.0625, ((0, 2),))
    adapter_down_weight = centred(part_keys[2], (ADAPTER_COUNT, MODEL_WIDTH, ADAPTER_RANK), MODEL_WIDTH ** -0.5, 0.0625, ((0, 8), (1, 2)))
    adapter_up_weight = centred(part_keys[3], (ADAPTER_COUNT, ADAPTER_RANK, HEAD_SIZE), ADAPTER_RANK ** -0.5, 0.75, ((0, 8),))
    key_value_cache = draw_key_value_cache(jax.random.fold_in(jax.random.fold_in(seeds[10], part), 71), part)
    query = centred(part_keys[5], (2, ROWS, HQ * HEAD_SIZE), 1.0, 6.0, ((1, 8),))
    fresh_token_keys = centred(part_keys[6], (2, ROWS, HEAD_SIZE), 1.0, 6.0, ((1, 8),))
    adapter_per_row_keys = jax.random.split(jax.random.fold_in(part_keys[7], 1), ROWS // ROW_DEV)
    adapter_per_row_turns = jax.random.permutation(jax.random.fold_in(part_keys[7], 3), ROWS // ROW_DEV)
    adapter_per_row = jax.vmap(lambda own, number: assign_block(jax.random.fold_in(part_keys[7], 2), own, number, ROW_DEV, ADAPTER_COUNT, 1, CAP, 2))(adapter_per_row_keys, adapter_per_row_turns).reshape((ROWS, 1))
    cache_length = with_ends(jax.random.randint(part_keys[8], (ROWS,), 1, LEN + 1), jax.random.fold_in(part_keys[8], 1), 1, LEN).astype(jnp.int32)
    adapter_storage_index = jax.random.permutation(part_keys[9], ADAPTER_COUNT).astype(jnp.int32)
    return dict(hidden=hidden, value_projection_weight=value_projection_weight, adapter_down_weight=adapter_down_weight, adapter_up_weight=adapter_up_weight, key_value_cache=key_value_cache, query=query, fresh_token_keys=fresh_token_keys, adapter_per_row=adapter_per_row, cache_length=cache_length, adapter_storage_index=adapter_storage_index)


adapter_scale = 1.0


def reference(hidden, value_projection_weight, adapter_down_weight, adapter_up_weight, key_value_cache, query, fresh_token_keys, adapter_per_row, cache_length, adapter_storage_index):
    high = lax.Precision.HIGHEST
    held = adapter_storage_index[adapter_per_row[:, 0]].astype(jnp.int32)
    base = jnp.einsum('srd,dh->srh', hidden.astype(jnp.float32), value_projection_weight.astype(jnp.float32), precision=high)
    blocks_x = jnp.transpose(hidden.reshape(2, N_BATCH, ROW_DEV, MODEL_WIDTH), (1, 0, 2, 3))
    blocks_held = held.reshape(N_BATCH, ROW_DEV)

    def adapt(pair):
        block_x, held_block = pair
        down_matrix = adapter_down_weight[held_block].astype(jnp.float32)
        up_matrix = adapter_up_weight[held_block].astype(jnp.float32)
        shrink = jnp.einsum('srd,rdk->srk', block_x.astype(jnp.float32), down_matrix, precision=high)
        return adapter_scale * jnp.einsum('srk,rkh->srh', shrink, up_matrix, precision=high)

    delta = lax.map(adapt, (blocks_x, blocks_held))
    delta = jnp.transpose(delta, (1, 0, 2, 3)).reshape(2, ROWS, HEAD_SIZE)
    new_values = lax.optimization_barrier((base + delta).astype(jnp.bfloat16)).astype(jnp.float32)
    heads = query.astype(jnp.float32).reshape(2, ROWS, HQ, HEAD_SIZE)
    inverse = HEAD_SIZE ** -0.5
    keys = key_value_cache[:, :, :HEAD_SIZE].astype(jnp.float32)
    values = key_value_cache[:, :, HEAD_SIZE:].astype(jnp.float32)
    own_keys = fresh_token_keys.astype(jnp.float32)
    cache_ok = (jnp.arange(LEN, dtype=jnp.int32)[None, :] < cache_length[:, None])[None, :, None, :]
    cache_scores = jnp.einsum('srhd,rld->srhl', heads, keys, precision=high) * inverse
    new_ok = (jnp.arange(2, dtype=jnp.int32)[None, :] <= jnp.arange(2, dtype=jnp.int32)[:, None])[:, None, None, :]
    new_scores = jnp.einsum('srhd,jrd->srhj', heads, own_keys, precision=high) * inverse
    cache_masked = jnp.where(cache_ok, cache_scores, -1e30)
    new_masked = jnp.where(new_ok, new_scores, -1e30)
    peak = jnp.maximum(jnp.max(cache_masked, axis=-1), jnp.max(new_masked, axis=-1))
    cache_weights = jnp.where(cache_ok, jnp.exp(cache_masked - peak[..., None]), 0.0)
    new_weights = jnp.where(new_ok, jnp.exp(new_masked - peak[..., None]), 0.0)
    total = jnp.sum(cache_weights, axis=-1) + jnp.sum(new_weights, axis=-1)
    cache_rounded = lax.optimization_barrier(cache_weights.astype(jnp.bfloat16)).astype(jnp.float32)
    new_rounded = lax.optimization_barrier(new_weights.astype(jnp.bfloat16)).astype(jnp.float32)
    summed = jnp.einsum('srhl,rld->srhd', cache_rounded, values, precision=high)
    summed = summed + jnp.einsum('srhj,jrd->srhd', new_rounded, new_values, precision=high)
    context = summed / total[..., None]
    return context.reshape(2, ROWS, HQ * HEAD_SIZE).astype(jnp.bfloat16)
```

```python
import jax
import jax.numpy as jnp
from jax import lax
from jax.experimental import pallas as pl
from jax.experimental.pallas import tpu as pltpu
from jax.sharding import PartitionSpec as P

HEAD_SIZE = 128
HQ = 8


adapter_scale = 1.0


def merged_2(array, axis, combine):
    everything = jax.tree.map(
        lambda part, kind: lax.all_gather(part.astype(kind), axis),
        array,
        (jnp.bfloat16, jnp.bfloat16, jnp.bfloat16),
    )

    def take(k):
        return jax.tree.map(lambda part, own: part[k].astype(own.dtype), everything, array)

    return lax.fori_loop(
        1, lax.axis_size(axis), lambda k, so_far: combine(so_far, take(k)), take(0)
    )


def combine(first, second):
    peak = jnp.maximum(first[0], second[0])
    left = jnp.exp(first[0] - peak)
    right = jnp.exp(second[0] - peak)
    return (
        peak,
        first[1] * left + second[1] * right,
        first[2] * left[..., None] + second[2] * right[..., None],
    )


def body(
    hidden,
    value_projection_weight,
    adapter_down_weight,
    adapter_up_weight,
    key_value_cache,
    query,
    fresh_token_keys,
    adapter_per_row,
    cache_length,
    adapter_storage_index,
):
    high = lax.Precision.HIGHEST
    nsteps, rows, half = hidden.shape
    peers = lax.axis_size("batch")
    slots = max(2, rows // peers)
    adapter = adapter_per_row[:, 0]
    count = adapter_storage_index.shape[0]
    match = adapter[:, None] == jnp.arange(count, dtype=jnp.int32)[None, :]
    held = jnp.sum(jnp.where(match, adapter_storage_index[None, :], 0), axis=1)
    onehot = (held[:, None] == jnp.arange(peers, dtype=jnp.int32)[None, :]).astype(jnp.int32)
    before = jnp.cumsum(onehot, axis=0) - onehot
    place = jnp.sum(before * onehot, axis=1)
    target = held * slots + place
    outgoing = jnp.zeros((nsteps, peers * slots, half), jnp.bfloat16).at[:, target].set(hidden)
    outgoing = outgoing.reshape(nsteps, peers, slots, half)
    local_down_matrix = adapter_down_weight[0]
    partial_shrink = jnp.einsum(
        "snkd,dr->snkr",
        lax.all_to_all(outgoing, "batch", split_axis=1, concat_axis=1, tiled=True),
        local_down_matrix,
        preferred_element_type=jnp.float32,
    )
    returned = lax.all_to_all(
        partial_shrink.astype(jnp.bfloat16), "batch", split_axis=1, concat_axis=1, tiled=True
    ).astype(partial_shrink.dtype)
    width = returned.shape[-1]
    per_row = returned.reshape(nsteps, peers * slots, width)[:, target]
    base_part = jnp.einsum(
        "srd,dh->srh", hidden, value_projection_weight, preferred_element_type=jnp.float32
    )
    adapter_tables = lax.all_gather(adapter_up_weight, "batch", axis=0, tiled=True)
    up_rows = adapter_tables[held].astype(jnp.float32)
    summand = base_part + adapter_scale * jnp.einsum(
        "srk,rkh->srh", per_row, up_rows, precision=high
    )
    new_value = lax.psum(summand.astype(jnp.bfloat16), "tensor")
    heads = query.reshape(nsteps, rows, HQ, HEAD_SIZE)
    inverse = HEAD_SIZE ** (-0.5)
    local_len = key_value_cache.shape[1]
    offset = lax.axis_index("tensor") * local_len
    positions = offset + jnp.arange(local_len, dtype=jnp.int32)
    cache_ok = (positions[None, :] < cache_length[:, None])[None, :, None, :]
    keys = key_value_cache[:, :, :HEAD_SIZE]
    values = key_value_cache[:, :, HEAD_SIZE:]
    scores = jnp.einsum("srhd,rld->srhl", heads, keys, preferred_element_type=jnp.float32) * inverse
    masked = jnp.where(cache_ok, scores, -1e30)
    peak = jnp.max(masked, axis=-1)
    weights = jnp.where(cache_ok, jnp.exp(masked - peak[..., None]), 0.0)
    total = jnp.sum(weights, axis=-1)
    summed = jnp.einsum(
        "srhl,rld->srhd", weights.astype(jnp.bfloat16), values, preferred_element_type=jnp.float32
    )
    merged = merged_2((peak, total, summed), "tensor", combine)
    steps_index = jnp.arange(2, dtype=jnp.int32)
    new_ok = (steps_index[None, :] <= steps_index[:, None])[:, None, None, :]
    own_scores = (
        jnp.einsum("srhd,jrd->srhj", heads, fresh_token_keys, preferred_element_type=jnp.float32)
        * inverse
    )
    own_masked = jnp.where(new_ok, own_scores, -1e30)
    own_peak = jnp.max(own_masked, axis=-1)
    own_weights = jnp.where(new_ok, jnp.exp(own_masked - own_peak[..., None]), 0.0)
    own_total = jnp.sum(own_weights, axis=-1)
    own_summed = jnp.einsum(
        "srhj,jrd->srhd",
        own_weights.astype(jnp.bfloat16),
        new_value,
        preferred_element_type=jnp.float32,
    )
    final = combine(merged, (own_peak, own_total, own_summed))
    context = final[2] / final[1][..., None]
    return context.reshape(nsteps, rows, HQ * HEAD_SIZE).astype(jnp.bfloat16)


SLOTS = 16
CHUNKS = 4
NT = (((1,), (1,)), ((), ()))
NN = (((1,), (0,)), ((), ()))


def mm(a, b, dims=NN):
    return lax.dot_general(a, b, dims, preferred_element_type=jnp.float32)


def halves(value):
    high = value.astype(jnp.bfloat16)
    low = (value - high.astype(jnp.float32)).astype(jnp.bfloat16)
    return high, low


def fused_kernel(
    hid, wv, down, up, cache, query, fresh, adapter, length, storage, out,
    hb, wvb, ab, ub, qb, kb, fb, grouped, from_x, from_end,
    deltas, to_x, to_end, base, vsend, vrecv, ctx, wnew, inv, lencol, unsort, nv,
    lsem, asend, arecv, csem, gsend, grecv, rrecv, dsend, drecv, vsem,
):
    group = lax.axis_index("group")
    me = lax.axis_index("batch")
    t = lax.axis_index("tensor")
    z, x = me // 2, me % 2
    pz = z + 1 - 2 * (z % 2)
    mid = ((z + 1) // 2) % 2
    is_mid = mid == 1
    is_end = mid == 0

    def dev(zz, xx):
        return (group, zz * 2 + xx, t)

    peer = (group, me, 1 - t)
    across = dev(z, 1 - x)
    beside = dev(pz, x)
    diagonal = dev(pz, 1 - x)
    far = dev(3 - z, x)
    onward = dev(pz + mid * (3 - z - pz), x)

    def remote(src, dst, send, recv, to):
        return pltpu.make_async_remote_copy(
            src_ref=src, dst_ref=dst, send_sem=send, recv_sem=recv,
            device_id=to, device_id_type=pl.DeviceIdType.MESH,
        )

    width = hb.shape[2]
    step = width // CHUNKS
    half_len = cache.shape[0]

    local = [
        pltpu.make_async_copy(hid, hb, lsem.at[0]),
        pltpu.make_async_copy(wv, wvb, lsem.at[1]),
        pltpu.make_async_copy(query, qb, lsem.at[2]),
        pltpu.make_async_copy(fresh, fb, lsem.at[3]),
        pltpu.make_async_copy(cache, kb.at[t], lsem.at[4]),
        pltpu.make_async_copy(down, ab.at[0], lsem.at[5]),
        pltpu.make_async_copy(up, ub.at[0], lsem.at[6]),
    ]
    for copy in local:
        copy.start()

    barrier = pltpu.get_barrier_semaphore()
    for to in (peer, across, beside, diagonal):
        pl.semaphore_signal(barrier, inc=1, device_id=to, device_id_type=pl.DeviceIdType.MESH)

    @pl.when(is_mid)
    def _():
        pl.semaphore_signal(barrier, inc=1, device_id=far, device_id_type=pl.DeviceIdType.MESH)

    pl.semaphore_wait(barrier, 4 + mid)

    def piece(slot, k):
        if k == 0:
            return ub.at[slot]
        return ab.at[slot, :, pl.ds((k - 1) * step, step)]

    def own_piece(k):
        return up if k == 0 else down.at[:, pl.ds((k - 1) * step, step)]

    pieces = range(CHUNKS + 1)
    own_out = [
        remote(own_piece(k), piece(1 + mid, k), asend.at[0, k], arecv.at[1 + mid, k], onward)
        for k in pieces
    ]
    for copy in own_out:
        copy.start()
    cache_out = remote(cache, kb.at[t], csem.at[0], csem.at[1], peer)
    cache_out.start()

    def forward(slot, k):
        to, there = {1: (far, 3), 2: (beside, 2), 3: (beside, 3)}[slot]
        return remote(piece(slot, k), piece(there, k), asend.at[slot, k], arecv.at[there, k], to)

    def arrived(slot, k):
        remote(piece(slot, k), piece(slot, k), asend.at[slot, k], arecv.at[slot, k], peer).wait_recv()

    def relay(k, slots):
        @pl.when(is_mid)
        def _():
            for slot in slots:
                arrived(slot, k)
                forward(slot, k).start()

    names = adapter[...]
    held = jnp.zeros_like(names)
    for a in range(storage.shape[0]):
        held = held + jnp.where(names == a, storage[a], 0)
    rows = names.shape[1]
    sub = lax.broadcasted_iota(jnp.int32, (rows, rows), 0)
    lane = lax.broadcasted_iota(jnp.int32, (rows, rows), 1)
    mine = lax.broadcasted_iota(jnp.int32, (8, rows), 0) == held
    earlier = mm(mine.astype(jnp.bfloat16), (sub < lane).astype(jnp.bfloat16))
    place = jnp.sum(jnp.where(mine, earlier, 0.0), axis=0, keepdims=True).astype(jnp.int32)
    hz = lax.shift_right_logical(held, 1)
    xrel = (held + x) & 1
    outer = jnp.where((hz == 1) | (hz == 2), 2, 3)
    same_side = lax.shift_right_logical(hz, 1) == z // 2
    relation = jnp.where(hz == z, 0, jnp.where(same_side, 1, outer))
    target = (relation * 2 + xrel) * SLOTS + place
    sort = (sub == target).astype(jnp.bfloat16)
    diag = sub == lane
    column = jnp.sum(jnp.where(diag, target, 0), axis=1, keepdims=True)
    unsort[...] = (column == lane).astype(jnp.bfloat16)
    lencol[...] = jnp.sum(jnp.where(diag, length[...], 0), axis=1, keepdims=True)

    local[0].wait()
    for k in range(CHUNKS):
        cols = pl.ds(k * step, step)
        for s in range(2):
            moved = mm(sort, hb[s, :, cols]).astype(jnp.bfloat16)
            for g in range(8):
                grouped[g, s * SLOTS:(s + 1) * SLOTS, cols] = moved[g * SLOTS:(g + 1) * SLOTS]

    def rows_across(q):
        return remote(grouped.at[2 * q + 1], from_x.at[q], gsend.at[2 * q + 1], grecv.at[q], across)

    rows_beside = remote(grouped.at[2], from_end.at[0], gsend.at[2], rrecv.at[0], beside)
    rows_diagonal = remote(grouped.at[3], from_end.at[1], gsend.at[3], rrecv.at[1], diagonal)
    rows_across(0).start()
    rows_across(2).start()

    @pl.when(is_mid)
    def _():
        rows_across(1).start()

    @pl.when(is_end)
    def _():
        rows_beside.start()
        rows_diagonal.start()

    rows_across(3).start()
    relay(0, (2, 1))

    local[1].wait()
    for s in range(2):
        base[s] = mm(hb[s], wvb[...])
    relay(1, (2, 1))

    for copy in local[2:]:
        copy.wait()
    cache_out.wait_recv()
    positions = half_len // rows
    cached = 2 * positions * SLOTS
    inverse = HEAD_SIZE ** (-0.5)

    def attend(b, carry):
        at = pl.ds(pl.multiple_of(b * SLOTS, SLOTS), SLOTS)
        cat = pl.ds(pl.multiple_of(b * SLOTS * positions, SLOTS * positions), SLOTS * positions)
        q = jnp.concatenate(
            [qb[s, at, h * HEAD_SIZE:(h + 1) * HEAD_SIZE] for s in range(2) for h in range(HQ)], axis=0
        )
        keys = jnp.concatenate(
            [kb[0, cat, :HEAD_SIZE], kb[1, cat, :HEAD_SIZE], fb[0, at, :], fb[1, at, :]], axis=0
        )
        scores = mm(q, keys, NT) * inverse
        i = lax.broadcasted_iota(jnp.int32, scores.shape, 0)
        c = lax.broadcasted_iota(jnp.int32, scores.shape, 1)
        per_half = SLOTS * positions
        in_cache = c < cached
        row_of = jnp.where(in_cache, (c % per_half) // positions, c % SLOTS)
        position = (c // per_half) * positions + c % positions
        limits = jnp.concatenate([lencol[at, :]] * (2 * HQ), axis=0)
        order = jnp.where(in_cache, position, (c - cached) // SLOTS)
        bound = jnp.where(in_cache, limits, i // (SLOTS * HQ) + 1)
        ok = (order < bound) & (row_of == i % SLOTS)
        masked = jnp.where(ok, scores, -1e30)
        peak = jnp.max(masked, axis=1, keepdims=True)
        weights = jnp.where(ok, jnp.exp(masked - peak), 0.0)
        inv[b] = 1.0 / jnp.sum(weights, axis=1, keepdims=True)
        rounded = weights.astype(jnp.bfloat16)
        values = jnp.concatenate([kb[0, cat, HEAD_SIZE:], kb[1, cat, HEAD_SIZE:]], axis=0)
        ctx[b] = mm(rounded[:, :cached], values)
        wnew[b] = rounded[:, cached:]
        return carry

    blocks = rows // SLOTS
    lax.fori_loop(0, 3, attend, 0)
    relay(2, (2, 1))
    lax.fori_loop(3, 6, attend, 0)
    relay(3, (2, 1))
    lax.fori_loop(6, blocks, attend, 0)
    relay(4, (2, 1))

    def project(first, second, slot, cols, so_far):
        both = jnp.concatenate([first[:, cols], second[:, cols]], axis=0)
        part = mm(both, ab[slot, :, cols], NT)
        return part if so_far is None else so_far + part

    def expand(shrink, slot):
        high, low = halves(shrink)
        return mm(high, ub[slot]) + mm(low, ub[slot])

    def delta_out(q):
        return remote(to_x.at[q], deltas.at[2 * q + 1], dsend.at[q], drecv.at[2 * q + 1], across)

    def finish(q, slot, shrink):
        delta = expand(shrink, slot)
        deltas[2 * q] = delta[:2 * SLOTS]
        to_x[q] = delta[2 * SLOTS:]
        delta_out(q).start()

    def relation_of(q, each=None):
        rows_across(q).wait_recv()
        shrink = None
        for k in range(CHUNKS):
            if each is not None:
                each(k)
            shrink = project(grouped.at[2 * q], from_x.at[q], q, pl.ds(k * step, step), shrink)
        finish(q, q, shrink)

    relation_of(0)

    @pl.when(is_end)
    def _():
        for k in pieces:
            arrived(2, k)

    relation_of(2)

    @pl.when(is_mid)
    def _():
        relation_of(1)
        for k in pieces:
            arrived(3, k)
            forward(3, k).start()

    result_beside = remote(to_end.at[0], deltas.at[2], dsend.at[4], drecv.at[2], beside)
    result_diagonal = remote(to_end.at[1], deltas.at[3], dsend.at[5], drecv.at[3], diagonal)

    @pl.when(is_mid)
    def _():
        rows_beside.wait_recv()
        rows_diagonal.wait_recv()
        shrink = None
        for k in range(CHUNKS):
            shrink = project(from_end.at[0], from_end.at[1], 0, pl.ds(k * step, step), shrink)
        delta = expand(shrink, 0)
        to_end[0] = delta[:2 * SLOTS]
        to_end[1] = delta[2 * SLOTS:]
        result_beside.start()
        result_diagonal.start()
        relation_of(3)

    @pl.when(is_end)
    def _():
        arrived(3, 0)
        relation_of(3, lambda k: arrived(3, k + 1))
        result_beside.wait_recv()
        result_diagonal.wait_recv()

    @pl.when(is_mid)
    def _():
        delta_out(1).wait_recv()

    for q in (0, 2, 3):
        delta_out(q).wait_recv()

    for s in range(2):
        ordered = jnp.concatenate([deltas[g, s * SLOTS:(s + 1) * SLOTS, :] for g in range(8)], axis=0)
        high, low = halves(ordered)
        vsend[s] = base[s] + adapter_scale * (mm(unsort[...], high) + mm(unsort[...], low))
    value_out = remote(vsend, vrecv, vsem.at[0], vsem.at[1], peer)
    value_out.start()
    value_out.wait_recv()
    nv[...] = (vsend[...] + vrecv[...]).astype(jnp.bfloat16)

    def close(b, carry):
        at = pl.ds(pl.multiple_of(b * SLOTS, SLOTS), SLOTS)
        fresh_values = jnp.concatenate([nv[0, at, :], nv[1, at, :]], axis=0)
        result = ((ctx[b] + mm(wnew[b], fresh_values)) * inv[b]).astype(out.dtype)
        for s in range(2):
            for h in range(HQ):
                first = (s * HQ + h) * SLOTS
                out[s, at, h * HEAD_SIZE:(h + 1) * HEAD_SIZE] = result[first:first + SLOTS]
        return carry

    lax.fori_loop(0, blocks, close, 0)

    value_out.wait_send()
    cache_out.wait_send()
    for copy in own_out:
        copy.wait_send()
    for q in (0, 2, 3):
        rows_across(q).wait_send()
        delta_out(q).wait_send()

    @pl.when(is_end)
    def _():
        rows_beside.wait_send()
        rows_diagonal.wait_send()

    @pl.when(is_mid)
    def _():
        rows_across(1).wait_send()
        delta_out(1).wait_send()
        result_beside.wait_send()
        result_diagonal.wait_send()
        for slot in (1, 2, 3):
            for k in pieces:
                forward(slot, k).wait_send()


def fused_body(
    hidden,
    value_projection_weight,
    adapter_down_weight,
    adapter_up_weight,
    key_value_cache,
    query,
    fresh_token_keys,
    adapter_per_row,
    cache_length,
    adapter_storage_index,
):
    bf16, f32 = jnp.bfloat16, jnp.float32
    _, rows, width = hidden.shape
    rank = adapter_down_weight.shape[2]
    local_len = key_value_cache.shape[1]
    down = jnp.swapaxes(adapter_down_weight[0], 0, 1)
    cache = key_value_cache.reshape(rows * local_len, 2 * HEAD_SIZE)
    blocks, tall = rows // SLOTS, 2 * HQ * SLOTS
    anywhere = pl.BlockSpec(memory_space=pl.ANY)
    vmem = pl.BlockSpec(memory_space=pltpu.VMEM)
    dma = pltpu.SemaphoreType.DMA
    return pl.pallas_call(
        fused_kernel,
        out_shape=jax.ShapeDtypeStruct(query.shape, bf16),
        in_specs=[anywhere] * 7 + [vmem, vmem, pl.BlockSpec(memory_space=pltpu.SMEM)],
        out_specs=vmem,
        scratch_shapes=[
            pltpu.VMEM(hidden.shape, bf16),
            pltpu.VMEM((width, HEAD_SIZE), bf16),
            pltpu.VMEM((4, rank, width), bf16),
            pltpu.VMEM((4, rank, HEAD_SIZE), bf16),
            pltpu.VMEM(query.shape, bf16),
            pltpu.VMEM((2,) + cache.shape, bf16),
            pltpu.VMEM(fresh_token_keys.shape, bf16),
            pltpu.VMEM((8, 2 * SLOTS, width), bf16),
            pltpu.VMEM((4, 2 * SLOTS, width), bf16),
            pltpu.VMEM((2, 2 * SLOTS, width), bf16),
            pltpu.VMEM((8, 2 * SLOTS, HEAD_SIZE), f32),
            pltpu.VMEM((4, 2 * SLOTS, HEAD_SIZE), f32),
            pltpu.VMEM((2, 2 * SLOTS, HEAD_SIZE), f32),
            pltpu.VMEM((2, rows, HEAD_SIZE), f32),
            pltpu.VMEM((2, rows, HEAD_SIZE), f32),
            pltpu.VMEM((2, rows, HEAD_SIZE), f32),
            pltpu.VMEM((blocks, tall, HEAD_SIZE), f32),
            pltpu.VMEM((blocks, tall, 2 * SLOTS), bf16),
            pltpu.VMEM((blocks, tall, 1), f32),
            pltpu.VMEM((rows, 1), jnp.int32),
            pltpu.VMEM((rows, rows), bf16),
            pltpu.VMEM((2, rows, HEAD_SIZE), bf16),
            dma((7,)),
            dma((4, CHUNKS + 1)),
            dma((4, CHUNKS + 1)),
            dma((2,)),
            dma((8,)),
            dma((4,)),
            dma((2,)),
            dma((6,)),
            dma((8,)),
            dma((2,)),
        ],
        compiler_params=pltpu.CompilerParams(
            collective_id=0, has_side_effects=True, vmem_limit_bytes=40 * 1024 * 1024
        ),
        cost_estimate=pl.CostEstimate(
            flops=2 * 4 * rows * width * HEAD_SIZE, bytes_accessed=6 << 20, transcendentals=rows * 2560
        ),
    )(
        hidden,
        value_projection_weight,
        down,
        adapter_up_weight[0],
        cache,
        query,
        fresh_token_keys,
        adapter_per_row.reshape(1, rows),
        cache_length.reshape(1, rows),
        adapter_storage_index,
    )


def solution(mesh):
    in_specs = (
        P(None, ("group", "batch"), "tensor"),
        P("tensor", None),
        P(("group", "batch"), "tensor", None),
        P(("group", "batch"), None, None),
        P(("group", "batch"), "tensor", None),
        P(None, ("group", "batch"), None),
        P(None, ("group", "batch"), None),
        P(("group", "batch"), None),
        P(("group", "batch")),
        P("group"),
    )
    out_specs = P(None, ("group", "batch"), None)
    small = mesh.shape["batch"] == 8 and mesh.shape["tensor"] == 2
    chosen = fused_body if small else body
    return jax.shard_map(chosen, mesh=mesh, in_specs=in_specs, out_specs=out_specs, check_vma=False)
```

```python
import jax
import jax.numpy as jnp
from jax import lax
from jax.experimental import pallas as pl
from jax.experimental.pallas import tpu as pltpu
from jax.sharding import PartitionSpec as P

HEAD_SIZE = 128
HQ = 8


adapter_scale = 1.0


def merged_2(array, axis, combine):
    everything = jax.tree.map(
        lambda part, kind: lax.all_gather(part.astype(kind), axis),
        array,
        (jnp.bfloat16, jnp.bfloat16, jnp.bfloat16),
    )

    def take(k):
        return jax.tree.map(lambda part, own: part[k].astype(own.dtype), everything, array)

    return lax.fori_loop(
        1, lax.axis_size(axis), lambda k, so_far: combine(so_far, take(k)), take(0)
    )


def combine(first, second):
    peak = jnp.maximum(first[0], second[0])
    left = jnp.exp(first[0] - peak)
    right = jnp.exp(second[0] - peak)
    return (
        peak,
        first[1] * left + second[1] * right,
        first[2] * left[..., None] + second[2] * right[..., None],
    )


def body(
    hidden,
    value_projection_weight,
    adapter_down_weight,
    adapter_up_weight,
    key_value_cache,
    query,
    fresh_token_keys,
    adapter_per_row,
    cache_length,
    adapter_storage_index,
):
    high = lax.Precision.HIGHEST
    nsteps, rows, half = hidden.shape
    peers = lax.axis_size("batch")
    slots = max(2, rows // peers)
    adapter = adapter_per_row[:, 0]
    count = adapter_storage_index.shape[0]
    match = adapter[:, None] == jnp.arange(count, dtype=jnp.int32)[None, :]
    held = jnp.sum(jnp.where(match, adapter_storage_index[None, :], 0), axis=1)
    onehot = (held[:, None] == jnp.arange(peers, dtype=jnp.int32)[None, :]).astype(jnp.int32)
    before = jnp.cumsum(onehot, axis=0) - onehot
    place = jnp.sum(before * onehot, axis=1)
    target = held * slots + place
    outgoing = jnp.zeros((nsteps, peers * slots, half), jnp.bfloat16).at[:, target].set(hidden)
    outgoing = outgoing.reshape(nsteps, peers, slots, half)
    local_down_matrix = adapter_down_weight[0]
    partial_shrink = jnp.einsum(
        "snkd,dr->snkr",
        lax.all_to_all(outgoing, "batch", split_axis=1, concat_axis=1, tiled=True),
        local_down_matrix,
        preferred_element_type=jnp.float32,
    )
    returned = lax.all_to_all(
        partial_shrink.astype(jnp.bfloat16), "batch", split_axis=1, concat_axis=1, tiled=True
    ).astype(partial_shrink.dtype)
    width = returned.shape[-1]
    per_row = returned.reshape(nsteps, peers * slots, width)[:, target]
    base_part = jnp.einsum(
        "srd,dh->srh", hidden, value_projection_weight, preferred_element_type=jnp.float32
    )
    adapter_tables = lax.all_gather(adapter_up_weight, "batch", axis=0, tiled=True)
    up_rows = adapter_tables[held].astype(jnp.float32)
    summand = base_part + adapter_scale * jnp.einsum(
        "srk,rkh->srh", per_row, up_rows, precision=high
    )
    new_value = lax.psum(summand.astype(jnp.bfloat16), "tensor")
    heads = query.reshape(nsteps, rows, HQ, HEAD_SIZE)
    inverse = HEAD_SIZE ** (-0.5)
    local_len = key_value_cache.shape[1]
    offset = lax.axis_index("tensor") * local_len
    positions = offset + jnp.arange(local_len, dtype=jnp.int32)
    cache_ok = (positions[None, :] < cache_length[:, None])[None, :, None, :]
    keys = key_value_cache[:, :, :HEAD_SIZE]
    values = key_value_cache[:, :, HEAD_SIZE:]
    scores = jnp.einsum("srhd,rld->srhl", heads, keys, preferred_element_type=jnp.float32) * inverse
    masked = jnp.where(cache_ok, scores, -1e30)
    peak = jnp.max(masked, axis=-1)
    weights = jnp.where(cache_ok, jnp.exp(masked - peak[..., None]), 0.0)
    total = jnp.sum(weights, axis=-1)
    summed = jnp.einsum(
        "srhl,rld->srhd", weights.astype(jnp.bfloat16), values, preferred_element_type=jnp.float32
    )
    merged = merged_2((peak, total, summed), "tensor", combine)
    steps_index = jnp.arange(2, dtype=jnp.int32)
    new_ok = (steps_index[None, :] <= steps_index[:, None])[:, None, None, :]
    own_scores = (
        jnp.einsum("srhd,jrd->srhj", heads, fresh_token_keys, preferred_element_type=jnp.float32)
        * inverse
    )
    own_masked = jnp.where(new_ok, own_scores, -1e30)
    own_peak = jnp.max(own_masked, axis=-1)
    own_weights = jnp.where(new_ok, jnp.exp(own_masked - own_peak[..., None]), 0.0)
    own_total = jnp.sum(own_weights, axis=-1)
    own_summed = jnp.einsum(
        "srhj,jrd->srhd",
        own_weights.astype(jnp.bfloat16),
        new_value,
        preferred_element_type=jnp.float32,
    )
    final = combine(merged, (own_peak, own_total, own_summed))
    context = final[2] / final[1][..., None]
    return context.reshape(nsteps, rows, HQ * HEAD_SIZE).astype(jnp.bfloat16)


SLOTS = 16
CHUNKS = 4
NT = (((1,), (1,)), ((), ()))
NN = (((1,), (0,)), ((), ()))


def mm(a, b, dims=NN):
    return lax.dot_general(a, b, dims, preferred_element_type=jnp.float32)


def halves(value):
    high = value.astype(jnp.bfloat16)
    low = (value - high.astype(jnp.float32)).astype(jnp.bfloat16)
    return high, low


def fused_kernel(
    hid, wv, down, up, cache, query, fresh, adapter_in, length_in, storage_in, out,
    adapter, length, storage,
    hb, wvb, ab, ub, qb, kb, fb, grouped, from_x, from_end,
    deltas, to_x, to_end, base, vsend, vrecv, ctx, wnew, inv, lencol, unsort, nv,
    lsem, asend, arecv, csem, gsend, grecv, rrecv, dsend, drecv, vsem,
):
    group = lax.axis_index("group")
    me = lax.axis_index("batch")
    t = lax.axis_index("tensor")
    z, x = me // 2, me % 2
    pz = z + 1 - 2 * (z % 2)
    mid = ((z + 1) // 2) % 2
    is_mid = mid == 1
    is_end = mid == 0

    def dev(zz, xx):
        return (group, zz * 2 + xx, t)

    peer = (group, me, 1 - t)
    across = dev(z, 1 - x)
    beside = dev(pz, x)
    diagonal = dev(pz, 1 - x)
    far = dev(3 - z, x)
    onward = dev(pz + mid * (3 - z - pz), x)

    def remote(src, dst, send, recv, to):
        return pltpu.make_async_remote_copy(
            src_ref=src, dst_ref=dst, send_sem=send, recv_sem=recv,
            device_id=to, device_id_type=pl.DeviceIdType.MESH,
        )

    width = hb.shape[2]
    step = width // CHUNKS
    half_len = cache.shape[0]

    local = [
        pltpu.make_async_copy(adapter_in, adapter, lsem.at[7]),
        pltpu.make_async_copy(length_in, length, lsem.at[8]),
        pltpu.make_async_copy(storage_in, storage, lsem.at[9]),
        pltpu.make_async_copy(hid, hb, lsem.at[0]),
        pltpu.make_async_copy(wv, wvb, lsem.at[1]),
        pltpu.make_async_copy(query, qb, lsem.at[2]),
        pltpu.make_async_copy(fresh, fb, lsem.at[3]),
        pltpu.make_async_copy(cache, kb.at[t], lsem.at[4]),
        pltpu.make_async_copy(down, ab.at[0], lsem.at[5]),
        pltpu.make_async_copy(up, ub.at[0], lsem.at[6]),
    ]
    for copy in local:
        copy.start()

    barrier = pltpu.get_barrier_semaphore()
    for to in (peer, across, beside, diagonal):
        pl.semaphore_signal(barrier, inc=1, device_id=to, device_id_type=pl.DeviceIdType.MESH)

    @pl.when(is_mid)
    def _():
        pl.semaphore_signal(barrier, inc=1, device_id=far, device_id_type=pl.DeviceIdType.MESH)

    pl.semaphore_wait(barrier, 4 + mid)

    def piece(slot, k):
        if k == CHUNKS:
            return ub.at[slot]
        return ab.at[slot, :, pl.ds(k * step, step)]

    def own_out(k):
        src = up if k == CHUNKS else down.at[:, pl.ds(k * step, step)]
        return remote(src, piece(1 + mid, k), asend.at[0, k], arecv.at[1 + mid, k], onward)

    pieces = range(CHUNKS + 1)
    own_out(CHUNKS).start()
    own_out(0).start()
    own_out(1).start()
    cache_out = remote(cache, kb.at[t], csem.at[0], csem.at[1], peer)
    cache_out.start()

    def forward(slot, k):
        to, there = {1: (far, 3), 2: (beside, 2), 3: (beside, 3)}[slot]
        return remote(piece(slot, k), piece(there, k), asend.at[slot, k], arecv.at[there, k], to)

    def arrived(slot, k):
        remote(piece(slot, k), piece(slot, k), asend.at[slot, k], arecv.at[slot, k], peer).wait_recv()

    def relay(slot, k):
        for j in ((CHUNKS, 0) if k == 0 else (k,)):
            arrived(slot, j)
            forward(slot, j).start()

    for copy in local[:3]:
        copy.wait()
    names = adapter[...]
    held = jnp.zeros_like(names)
    for a in range(storage.shape[0]):
        held = held + jnp.where(names == a, storage[a], 0)
    rows = names.shape[1]
    sub = lax.broadcasted_iota(jnp.int32, (rows, rows), 0)
    lane = lax.broadcasted_iota(jnp.int32, (rows, rows), 1)
    mine = lax.broadcasted_iota(jnp.int32, (8, rows), 0) == held
    earlier = mm(mine.astype(jnp.bfloat16), (sub < lane).astype(jnp.bfloat16))
    place = jnp.sum(jnp.where(mine, earlier, 0.0), axis=0, keepdims=True).astype(jnp.int32)
    hz = lax.shift_right_logical(held, 1)
    xrel = (held + x) & 1
    outer = jnp.where((hz == 1) | (hz == 2), 2, 3)
    same_side = lax.shift_right_logical(hz, 1) == z // 2
    relation = jnp.where(hz == z, 0, jnp.where(same_side, 1, outer))
    target = (relation * 2 + xrel) * SLOTS + place
    sort = (sub == target).astype(jnp.bfloat16)
    diag = sub == lane
    column = jnp.sum(jnp.where(diag, target, 0), axis=1, keepdims=True)
    unsort[...] = (column == lane).astype(jnp.bfloat16)
    lencol[...] = jnp.sum(jnp.where(diag, length[...], 0), axis=1, keepdims=True)

    local[3].wait()
    for k in range(CHUNKS):
        cols = pl.ds(k * step, step)
        for s in range(2):
            moved = mm(sort, hb[s, :, cols]).astype(jnp.bfloat16)
            for g in range(8):
                grouped[g, s * SLOTS:(s + 1) * SLOTS, cols] = moved[g * SLOTS:(g + 1) * SLOTS]

    def rows_across(q):
        return remote(grouped.at[2 * q + 1], from_x.at[q], gsend.at[2 * q + 1], grecv.at[q], across)

    rows_beside = remote(grouped.at[2], from_end.at[0], gsend.at[2], rrecv.at[0], beside)
    rows_diagonal = remote(grouped.at[3], from_end.at[1], gsend.at[3], rrecv.at[1], diagonal)
    rows_across(0).start()
    rows_across(2).start()

    @pl.when(is_mid)
    def _():
        relay(2, 0)
        own_out(2).start()

    @pl.when(is_end)
    def _():
        own_out(0).wait_send()
        own_out(2).start()

    local[4].wait()
    for s in range(2):
        base[s] = mm(hb[s], wvb[...])

    @pl.when(is_mid)
    def _():
        relay(2, 1)
        own_out(3).start()

    @pl.when(is_end)
    def _():
        own_out(1).wait_send()
        own_out(3).start()

    for copy in local[5:]:
        copy.wait()
    cache_out.wait_recv()
    positions = half_len // rows
    cached = 2 * positions * SLOTS
    inverse = HEAD_SIZE ** (-0.5)

    def attend(b, carry):
        at = pl.ds(pl.multiple_of(b * SLOTS, SLOTS), SLOTS)
        cat = pl.ds(pl.multiple_of(b * SLOTS * positions, SLOTS * positions), SLOTS * positions)
        q = jnp.concatenate(
            [qb[s, at, h * HEAD_SIZE:(h + 1) * HEAD_SIZE] for s in range(2) for h in range(HQ)], axis=0
        )
        keys = jnp.concatenate(
            [kb[0, cat, :HEAD_SIZE], kb[1, cat, :HEAD_SIZE], fb[0, at, :], fb[1, at, :]], axis=0
        )
        scores = mm(q, keys, NT) * inverse
        i = lax.broadcasted_iota(jnp.int32, scores.shape, 0)
        c = lax.broadcasted_iota(jnp.int32, scores.shape, 1)
        per_half = SLOTS * positions
        in_cache = c < cached
        row_of = jnp.where(in_cache, (c % per_half) // positions, c % SLOTS)
        position = (c // per_half) * positions + c % positions
        limits = jnp.concatenate([lencol[at, :]] * (2 * HQ), axis=0)
        order = jnp.where(in_cache, position, (c - cached) // SLOTS)
        bound = jnp.where(in_cache, limits, i // (SLOTS * HQ) + 1)
        ok = (order < bound) & (row_of == i % SLOTS)
        masked = jnp.where(ok, scores, -1e30)
        peak = jnp.max(masked, axis=1, keepdims=True)
        weights = jnp.where(ok, jnp.exp(masked - peak), 0.0)
        inv[b] = 1.0 / jnp.sum(weights, axis=1, keepdims=True)
        rounded = weights.astype(jnp.bfloat16)
        values = jnp.concatenate([kb[0, cat, HEAD_SIZE:], kb[1, cat, HEAD_SIZE:]], axis=0)
        ctx[b] = mm(rounded[:, :cached], values)
        wnew[b] = rounded[:, cached:]
        return carry

    blocks = rows // SLOTS
    lax.fori_loop(0, 3, attend, 0)

    @pl.when(is_mid)
    def _():
        relay(2, 2)
        relay(1, 0)
        rows_across(1).start()

    @pl.when(is_end)
    def _():
        own_out(2).wait_send()
        rows_beside.start()

    lax.fori_loop(3, 6, attend, 0)

    @pl.when(is_mid)
    def _():
        relay(2, 3)
        relay(1, 1)

    @pl.when(is_end)
    def _():
        own_out(3).wait_send()
        rows_diagonal.start()

    rows_across(3).start()
    lax.fori_loop(6, blocks, attend, 0)

    def project(first, second, slot, cols, so_far):
        both = jnp.concatenate([first[:, cols], second[:, cols]], axis=0)
        part = mm(both, ab[slot, :, cols], NT)
        return part if so_far is None else so_far + part

    def expand(shrink, slot):
        high, low = halves(shrink)
        return mm(high, ub[slot]) + mm(low, ub[slot])

    def delta_out(q):
        return remote(to_x.at[q], deltas.at[2 * q + 1], dsend.at[q], drecv.at[2 * q + 1], across)

    def finish(q, slot, shrink):
        delta = expand(shrink, slot)
        deltas[2 * q] = delta[:2 * SLOTS]
        to_x[q] = delta[2 * SLOTS:]
        delta_out(q).start()

    def relation_of(q, each=None):
        rows_across(q).wait_recv()
        shrink = None
        for k in range(CHUNKS):
            if each is not None:
                each(k)
            shrink = project(grouped.at[2 * q], from_x.at[q], q, pl.ds(k * step, step), shrink)
        finish(q, q, shrink)

    @pl.when(is_mid)
    def _():
        relay(1, 2)
        relay(3, 0)
        relay(1, 3)
        relay(3, 1)

    relation_of(0)

    @pl.when(is_mid)
    def _():
        relay(3, 2)

    @pl.when(is_end)
    def _():
        for k in pieces:
            arrived(2, k)

    relation_of(2)

    @pl.when(is_mid)
    def _():
        relay(3, 3)
        relation_of(1)

    result_beside = remote(to_end.at[0], deltas.at[2], dsend.at[4], drecv.at[2], beside)
    result_diagonal = remote(to_end.at[1], deltas.at[3], dsend.at[5], drecv.at[3], diagonal)

    @pl.when(is_mid)
    def _():
        rows_beside.wait_recv()
        rows_diagonal.wait_recv()
        shrink = None
        for k in range(CHUNKS):
            shrink = project(from_end.at[0], from_end.at[1], 0, pl.ds(k * step, step), shrink)
        delta = expand(shrink, 0)
        to_end[0] = delta[:2 * SLOTS]
        to_end[1] = delta[2 * SLOTS:]
        result_beside.start()
        result_diagonal.start()
        relation_of(3)

    @pl.when(is_end)
    def _():
        arrived(3, CHUNKS)
        relation_of(3, lambda k: arrived(3, k))
        result_beside.wait_recv()
        result_diagonal.wait_recv()

    @pl.when(is_mid)
    def _():
        delta_out(1).wait_recv()

    for q in (0, 2, 3):
        delta_out(q).wait_recv()

    for s in range(2):
        ordered = jnp.concatenate([deltas[g, s * SLOTS:(s + 1) * SLOTS, :] for g in range(8)], axis=0)
        high, low = halves(ordered)
        vsend[s] = base[s] + adapter_scale * (mm(unsort[...], high) + mm(unsort[...], low))
    value_out = remote(vsend, vrecv, vsem.at[0], vsem.at[1], peer)
    value_out.start()
    value_out.wait_recv()
    nv[...] = (vsend[...] + vrecv[...]).astype(jnp.bfloat16)

    def close(b, carry):
        at = pl.ds(pl.multiple_of(b * SLOTS, SLOTS), SLOTS)
        fresh_values = jnp.concatenate([nv[0, at, :], nv[1, at, :]], axis=0)
        result = ((ctx[b] + mm(wnew[b], fresh_values)) * inv[b]).astype(out.dtype)
        for s in range(2):
            for h in range(HQ):
                first = (s * HQ + h) * SLOTS
                out[s, at, h * HEAD_SIZE:(h + 1) * HEAD_SIZE] = result[first:first + SLOTS]
        return carry

    lax.fori_loop(0, blocks, close, 0)

    value_out.wait_send()
    cache_out.wait_send()
    own_out(CHUNKS).wait_send()
    for q in (0, 2, 3):
        rows_across(q).wait_send()
        delta_out(q).wait_send()

    @pl.when(is_end)
    def _():
        rows_beside.wait_send()
        rows_diagonal.wait_send()

    @pl.when(is_mid)
    def _():
        for k in range(CHUNKS):
            own_out(k).wait_send()
        rows_across(1).wait_send()
        delta_out(1).wait_send()
        result_beside.wait_send()
        result_diagonal.wait_send()
        for slot in (1, 2, 3):
            for k in pieces:
                forward(slot, k).wait_send()


def fused_body(
    hidden,
    value_projection_weight,
    adapter_down_weight,
    adapter_up_weight,
    key_value_cache,
    query,
    fresh_token_keys,
    adapter_per_row,
    cache_length,
    adapter_storage_index,
):
    bf16, f32 = jnp.bfloat16, jnp.float32
    _, rows, width = hidden.shape
    rank = adapter_down_weight.shape[2]
    local_len = key_value_cache.shape[1]
    down = jnp.swapaxes(adapter_down_weight[0], 0, 1)
    cache = key_value_cache.reshape(rows * local_len, 2 * HEAD_SIZE)
    blocks, tall = rows // SLOTS, 2 * HQ * SLOTS
    dma = pltpu.SemaphoreType.DMA
    return pl.pallas_call(
        fused_kernel,
        out_shape=jax.ShapeDtypeStruct(query.shape, bf16),
        in_specs=[pl.BlockSpec(memory_space=pltpu.HBM)] * 10,
        out_specs=pl.BlockSpec(memory_space=pltpu.VMEM),
        scratch_shapes=[
            pltpu.VMEM((1, rows), jnp.int32),
            pltpu.VMEM((1, rows), jnp.int32),
            pltpu.SMEM(adapter_storage_index.shape, jnp.int32),
            pltpu.VMEM(hidden.shape, bf16),
            pltpu.VMEM((width, HEAD_SIZE), bf16),
            pltpu.VMEM((4, rank, width), bf16),
            pltpu.VMEM((4, rank, HEAD_SIZE), bf16),
            pltpu.VMEM(query.shape, bf16),
            pltpu.VMEM((2,) + cache.shape, bf16),
            pltpu.VMEM(fresh_token_keys.shape, bf16),
            pltpu.VMEM((8, 2 * SLOTS, width), bf16),
            pltpu.VMEM((4, 2 * SLOTS, width), bf16),
            pltpu.VMEM((2, 2 * SLOTS, width), bf16),
            pltpu.VMEM((8, 2 * SLOTS, HEAD_SIZE), f32),
            pltpu.VMEM((4, 2 * SLOTS, HEAD_SIZE), f32),
            pltpu.VMEM((2, 2 * SLOTS, HEAD_SIZE), f32),
            pltpu.VMEM((2, rows, HEAD_SIZE), f32),
            pltpu.VMEM((2, rows, HEAD_SIZE), f32),
            pltpu.VMEM((2, rows, HEAD_SIZE), f32),
            pltpu.VMEM((blocks, tall, HEAD_SIZE), f32),
            pltpu.VMEM((blocks, tall, 2 * SLOTS), bf16),
            pltpu.VMEM((blocks, tall, 1), f32),
            pltpu.VMEM((rows, 1), jnp.int32),
            pltpu.VMEM((rows, rows), bf16),
            pltpu.VMEM((2, rows, HEAD_SIZE), bf16),
            dma((10,)),
            dma((4, CHUNKS + 1)),
            dma((4, CHUNKS + 1)),
            dma((2,)),
            dma((8,)),
            dma((4,)),
            dma((2,)),
            dma((6,)),
            dma((8,)),
            dma((2,)),
        ],
        compiler_params=pltpu.CompilerParams(
            collective_id=0, has_side_effects=True, vmem_limit_bytes=56 * 1024 * 1024
        ),
        cost_estimate=pl.CostEstimate(
            flops=2 * 4 * rows * width * HEAD_SIZE, bytes_accessed=6 << 20, transcendentals=rows * 2560
        ),
    )(
        hidden,
        value_projection_weight,
        down,
        adapter_up_weight[0],
        cache,
        query,
        fresh_token_keys,
        adapter_per_row.reshape(1, rows),
        cache_length.reshape(1, rows),
        adapter_storage_index,
    )


def solution(mesh):
    in_specs = (
        P(None, ("group", "batch"), "tensor"),
        P("tensor", None),
        P(("group", "batch"), "tensor", None),
        P(("group", "batch"), None, None),
        P(("group", "batch"), "tensor", None),
        P(None, ("group", "batch"), None),
        P(None, ("group", "batch"), None),
        P(("group", "batch"), None),
        P(("group", "batch")),
        P("group"),
    )
    out_specs = P(None, ("group", "batch"), None)
    small = mesh.shape["batch"] == 8 and mesh.shape["tensor"] == 2
    chosen = fused_body if small else body
    return jax.shard_map(chosen, mesh=mesh, in_specs=in_specs, out_specs=out_specs, check_vma=False)
```

```python
import jax
import jax.numpy as jnp
from jax import lax
from jax.experimental import pallas as pl
from jax.experimental.pallas import tpu as pltpu
from jax.sharding import PartitionSpec as P

HEAD_SIZE = 128
HQ = 8


adapter_scale = 1.0


def merged_2(array, axis, combine):
    everything = jax.tree.map(
        lambda part, kind: lax.all_gather(part.astype(kind), axis),
        array,
        (jnp.bfloat16, jnp.bfloat16, jnp.bfloat16),
    )

    def take(k):
        return jax.tree.map(lambda part, own: part[k].astype(own.dtype), everything, array)

    return lax.fori_loop(
        1, lax.axis_size(axis), lambda k, so_far: combine(so_far, take(k)), take(0)
    )


def combine(first, second):
    peak = jnp.maximum(first[0], second[0])
    left = jnp.exp(first[0] - peak)
    right = jnp.exp(second[0] - peak)
    return (
        peak,
        first[1] * left + second[1] * right,
        first[2] * left[..., None] + second[2] * right[..., None],
    )


def body(
    hidden,
    value_projection_weight,
    adapter_down_weight,
    adapter_up_weight,
    key_value_cache,
    query,
    fresh_token_keys,
    adapter_per_row,
    cache_length,
    adapter_storage_index,
):
    high = lax.Precision.HIGHEST
    nsteps, rows, half = hidden.shape
    peers = lax.axis_size("batch")
    slots = max(2, rows // peers)
    adapter = adapter_per_row[:, 0]
    count = adapter_storage_index.shape[0]
    match = adapter[:, None] == jnp.arange(count, dtype=jnp.int32)[None, :]
    held = jnp.sum(jnp.where(match, adapter_storage_index[None, :], 0), axis=1)
    onehot = (held[:, None] == jnp.arange(peers, dtype=jnp.int32)[None, :]).astype(jnp.int32)
    before = jnp.cumsum(onehot, axis=0) - onehot
    place = jnp.sum(before * onehot, axis=1)
    target = held * slots + place
    outgoing = jnp.zeros((nsteps, peers * slots, half), jnp.bfloat16).at[:, target].set(hidden)
    outgoing = outgoing.reshape(nsteps, peers, slots, half)
    local_down_matrix = adapter_down_weight[0]
    partial_shrink = jnp.einsum(
        "snkd,dr->snkr",
        lax.all_to_all(outgoing, "batch", split_axis=1, concat_axis=1, tiled=True),
        local_down_matrix,
        preferred_element_type=jnp.float32,
    )
    returned = lax.all_to_all(
        partial_shrink.astype(jnp.bfloat16), "batch", split_axis=1, concat_axis=1, tiled=True
    ).astype(partial_shrink.dtype)
    width = returned.shape[-1]
    per_row = returned.reshape(nsteps, peers * slots, width)[:, target]
    base_part = jnp.einsum(
        "srd,dh->srh", hidden, value_projection_weight, preferred_element_type=jnp.float32
    )
    adapter_tables = lax.all_gather(adapter_up_weight, "batch", axis=0, tiled=True)
    up_rows = adapter_tables[held].astype(jnp.float32)
    summand = base_part + adapter_scale * jnp.einsum(
        "srk,rkh->srh", per_row, up_rows, precision=high
    )
    new_value = lax.psum(summand.astype(jnp.bfloat16), "tensor")
    heads = query.reshape(nsteps, rows, HQ, HEAD_SIZE)
    inverse = HEAD_SIZE ** (-0.5)
    local_len = key_value_cache.shape[1]
    offset = lax.axis_index("tensor") * local_len
    positions = offset + jnp.arange(local_len, dtype=jnp.int32)
    cache_ok = (positions[None, :] < cache_length[:, None])[None, :, None, :]
    keys = key_value_cache[:, :, :HEAD_SIZE]
    values = key_value_cache[:, :, HEAD_SIZE:]
    scores = jnp.einsum("srhd,rld->srhl", heads, keys, preferred_element_type=jnp.float32) * inverse
    masked = jnp.where(cache_ok, scores, -1e30)
    peak = jnp.max(masked, axis=-1)
    weights = jnp.where(cache_ok, jnp.exp(masked - peak[..., None]), 0.0)
    total = jnp.sum(weights, axis=-1)
    summed = jnp.einsum(
        "srhl,rld->srhd", weights.astype(jnp.bfloat16), values, preferred_element_type=jnp.float32
    )
    merged = merged_2((peak, total, summed), "tensor", combine)
    steps_index = jnp.arange(2, dtype=jnp.int32)
    new_ok = (steps_index[None, :] <= steps_index[:, None])[:, None, None, :]
    own_scores = (
        jnp.einsum("srhd,jrd->srhj", heads, fresh_token_keys, preferred_element_type=jnp.float32)
        * inverse
    )
    own_masked = jnp.where(new_ok, own_scores, -1e30)
    own_peak = jnp.max(own_masked, axis=-1)
    own_weights = jnp.where(new_ok, jnp.exp(own_masked - own_peak[..., None]), 0.0)
    own_total = jnp.sum(own_weights, axis=-1)
    own_summed = jnp.einsum(
        "srhj,jrd->srhd",
        own_weights.astype(jnp.bfloat16),
        new_value,
        preferred_element_type=jnp.float32,
    )
    final = combine(merged, (own_peak, own_total, own_summed))
    context = final[2] / final[1][..., None]
    return context.reshape(nsteps, rows, HQ * HEAD_SIZE).astype(jnp.bfloat16)


SLOTS = 16
CHUNKS = 4
NT = (((1,), (1,)), ((), ()))
NN = (((1,), (0,)), ((), ()))


def mm(a, b, dims=NN):
    return lax.dot_general(a, b, dims, preferred_element_type=jnp.float32)


def halves(value):
    high = value.astype(jnp.bfloat16)
    low = (value - high.astype(jnp.float32)).astype(jnp.bfloat16)
    return high, low


def fused_kernel(
    hid, wv, down, up, cache, query, fresh, adapter_in, length_in, storage_in, out,
    adapter, length, storage,
    hb, wvb, ab, ub, qb, kb, fb, grouped, from_x, from_end,
    deltas, to_x, to_end, base, vsend, vrecv, ctx, wnew, inv, lencol, unsort, nv,
    lsem, asend, arecv, csem, gsend, grecv, rrecv, dsend, drecv, vsem,
):
    group = lax.axis_index("group")
    me = lax.axis_index("batch")
    t = lax.axis_index("tensor")
    z, x = me // 2, me % 2
    pz = z + 1 - 2 * (z % 2)
    mid = ((z + 1) // 2) % 2
    is_mid = mid == 1
    is_end = mid == 0

    def dev(zz, xx):
        return (group, zz * 2 + xx, t)

    peer = (group, me, 1 - t)
    across = dev(z, 1 - x)
    beside = dev(pz, x)
    diagonal = dev(pz, 1 - x)
    far = dev(3 - z, x)
    onward = dev(pz + mid * (3 - z - pz), x)

    def remote(src, dst, send, recv, to):
        return pltpu.make_async_remote_copy(
            src_ref=src, dst_ref=dst, send_sem=send, recv_sem=recv,
            device_id=to, device_id_type=pl.DeviceIdType.MESH,
        )

    width = hb.shape[2]
    step = width // CHUNKS
    positions = cache.shape[1]

    local = [
        pltpu.make_async_copy(adapter_in, adapter, lsem.at[7]),
        pltpu.make_async_copy(length_in, length, lsem.at[8]),
        pltpu.make_async_copy(storage_in, storage, lsem.at[9]),
        pltpu.make_async_copy(hid, hb, lsem.at[0]),
        pltpu.make_async_copy(wv, wvb, lsem.at[1]),
        pltpu.make_async_copy(query, qb, lsem.at[2]),
        pltpu.make_async_copy(fresh, fb, lsem.at[3]),
        pltpu.make_async_copy(cache, kb.at[t], lsem.at[4]),
        pltpu.make_async_copy(down, ab.at[0], lsem.at[5]),
        pltpu.make_async_copy(up, ub.at[0], lsem.at[6]),
    ]
    for copy in local:
        copy.start()

    barrier = pltpu.get_barrier_semaphore()
    for to in (peer, across, beside, diagonal):
        pl.semaphore_signal(barrier, inc=1, device_id=to, device_id_type=pl.DeviceIdType.MESH)

    @pl.when(is_mid)
    def _():
        pl.semaphore_signal(barrier, inc=1, device_id=far, device_id_type=pl.DeviceIdType.MESH)

    pl.semaphore_wait(barrier, 4 + mid)

    def piece(slot, k):
        if k == CHUNKS:
            return ub.at[slot]
        return ab.at[slot, :, pl.ds(k * step, step)]

    def own_out(k):
        src = up if k == CHUNKS else down.at[:, pl.ds(k * step, step)]
        return remote(src, piece(1 + mid, k), asend.at[0, k], arecv.at[1 + mid, k], onward)

    pieces = range(CHUNKS + 1)
    own_out(CHUNKS).start()
    own_out(0).start()
    own_out(1).start()
    cache_out = remote(cache, kb.at[t], csem.at[0], csem.at[1], peer)
    cache_out.start()

    def forward(slot, k):
        to, there = {1: (far, 3), 2: (beside, 2), 3: (beside, 3)}[slot]
        return remote(piece(slot, k), piece(there, k), asend.at[slot, k], arecv.at[there, k], to)

    def arrived(slot, k):
        remote(piece(slot, k), piece(slot, k), asend.at[slot, k], arecv.at[slot, k], peer).wait_recv()

    def relay(slot, k):
        for j in ((CHUNKS, 0) if k == 0 else (k,)):
            arrived(slot, j)
            forward(slot, j).start()

    for copy in local[:3]:
        copy.wait()
    names = adapter[...]
    held = jnp.zeros_like(names)
    for a in range(storage.shape[0]):
        held = held + jnp.where(names == a, storage[a], 0)
    rows = names.shape[1]
    sub = lax.broadcasted_iota(jnp.int32, (rows, rows), 0)
    lane = lax.broadcasted_iota(jnp.int32, (rows, rows), 1)
    mine = lax.broadcasted_iota(jnp.int32, (8, rows), 0) == held
    earlier = mm(mine.astype(jnp.bfloat16), (sub < lane).astype(jnp.bfloat16))
    place = jnp.sum(jnp.where(mine, earlier, 0.0), axis=0, keepdims=True).astype(jnp.int32)
    hz = lax.shift_right_logical(held, 1)
    xrel = (held + x) & 1
    outer = jnp.where((hz == 1) | (hz == 2), 2, 3)
    same_side = lax.shift_right_logical(hz, 1) == z // 2
    relation = jnp.where(hz == z, 0, jnp.where(same_side, 1, outer))
    target = (relation * 2 + xrel) * SLOTS + place
    sort = (sub == target).astype(jnp.bfloat16)
    diag = sub == lane
    column = jnp.sum(jnp.where(diag, target, 0), axis=1, keepdims=True)
    unsort[...] = (column == lane).astype(jnp.bfloat16)
    lencol[...] = jnp.sum(jnp.where(diag, length[...], 0), axis=1, keepdims=True)

    local[3].wait()
    for k in range(CHUNKS):
        cols = pl.ds(k * step, step)
        for s in range(2):
            moved = mm(sort, hb[s, :, cols]).astype(jnp.bfloat16)
            for g in range(8):
                grouped[g, s * SLOTS:(s + 1) * SLOTS, cols] = moved[g * SLOTS:(g + 1) * SLOTS]

    def rows_across(q):
        return remote(grouped.at[2 * q + 1], from_x.at[q], gsend.at[2 * q + 1], grecv.at[q], across)

    rows_beside = remote(grouped.at[2], from_end.at[0], gsend.at[2], rrecv.at[0], beside)
    rows_onward = remote(from_x.at[1], from_end.at[1], gsend.at[4], rrecv.at[1], beside)
    rows_across(0).start()

    @pl.when(is_end)
    def _():
        rows_across(1).start()

    @pl.when(is_mid)
    def _():
        rows_across(2).start()

    @pl.when(is_mid)
    def _():
        relay(2, 0)
        own_out(2).start()

    @pl.when(is_end)
    def _():
        own_out(0).wait_send()
        own_out(2).start()

    local[4].wait()
    for s in range(2):
        base[s] = mm(hb[s], wvb[...])

    @pl.when(is_mid)
    def _():
        relay(2, 1)
        own_out(3).start()
        rows_across(1).start()

    @pl.when(is_end)
    def _():
        own_out(1).wait_send()
        own_out(3).start()
        rows_across(2).start()

    for copy in local[5:]:
        copy.wait()
    cache_out.wait_recv()
    cached = 2 * positions * SLOTS
    inverse = HEAD_SIZE ** (-0.5)

    def attend(b, carry):
        at = pl.ds(pl.multiple_of(b * SLOTS, SLOTS), SLOTS)
        cached_rows = [
            kb[i, at].astype(jnp.float32).reshape(SLOTS * positions, 2 * HEAD_SIZE).astype(jnp.bfloat16)
            for i in range(2)
        ]
        q = jnp.concatenate(
            [qb[s, at, h * HEAD_SIZE:(h + 1) * HEAD_SIZE] for s in range(2) for h in range(HQ)], axis=0
        )
        keys = jnp.concatenate(
            [cached_rows[0][:, :HEAD_SIZE], cached_rows[1][:, :HEAD_SIZE], fb[0, at, :], fb[1, at, :]], axis=0
        )
        scores = mm(q, keys, NT) * inverse
        i = lax.broadcasted_iota(jnp.int32, scores.shape, 0)
        c = lax.broadcasted_iota(jnp.int32, scores.shape, 1)
        per_half = SLOTS * positions
        in_cache = c < cached
        row_of = jnp.where(in_cache, (c % per_half) // positions, c % SLOTS)
        position = (c // per_half) * positions + c % positions
        limits = jnp.concatenate([lencol[at, :]] * (2 * HQ), axis=0)
        order = jnp.where(in_cache, position, (c - cached) // SLOTS)
        bound = jnp.where(in_cache, limits, i // (SLOTS * HQ) + 1)
        ok = (order < bound) & (row_of == i % SLOTS)
        masked = jnp.where(ok, scores, -1e30)
        peak = jnp.max(masked, axis=1, keepdims=True)
        weights = jnp.where(ok, jnp.exp(masked - peak), 0.0)
        inv[b] = 1.0 / jnp.sum(weights, axis=1, keepdims=True)
        rounded = weights.astype(jnp.bfloat16)
        values = jnp.concatenate([cached_rows[0][:, HEAD_SIZE:], cached_rows[1][:, HEAD_SIZE:]], axis=0)
        ctx[b] = mm(rounded[:, :cached], values)
        wnew[b] = rounded[:, cached:]
        return carry

    blocks = rows // SLOTS
    lax.fori_loop(0, 3, attend, 0)

    @pl.when(is_mid)
    def _():
        relay(2, 2)
        relay(1, 0)

    @pl.when(is_end)
    def _():
        own_out(2).wait_send()
        rows_beside.start()

    rows_across(3).start()
    lax.fori_loop(3, 6, attend, 0)

    @pl.when(is_mid)
    def _():
        relay(2, 3)
        relay(1, 1)

    @pl.when(is_end)
    def _():
        own_out(3).wait_send()
        rows_across(1).wait_recv()
        rows_onward.start()

    lax.fori_loop(6, blocks, attend, 0)

    def project(first, second, slot, cols, so_far):
        both = jnp.concatenate([first[:, cols], second[:, cols]], axis=0)
        part = mm(both, ab[slot, :, cols], NT)
        return part if so_far is None else so_far + part

    def expand(shrink, slot):
        high, low = halves(shrink)
        return mm(high, ub[slot]) + mm(low, ub[slot])

    def delta_out(q):
        return remote(to_x.at[q], deltas.at[2 * q + 1], dsend.at[q], drecv.at[2 * q + 1], across)

    def finish(q, slot, shrink):
        delta = expand(shrink, slot)
        deltas[2 * q] = delta[:2 * SLOTS]
        to_x[q] = delta[2 * SLOTS:]
        delta_out(q).start()

    def relation_of(q, each=None):
        rows_across(q).wait_recv()
        shrink = None
        for k in range(CHUNKS):
            if each is not None:
                each(k)
            shrink = project(grouped.at[2 * q], from_x.at[q], q, pl.ds(k * step, step), shrink)
        finish(q, q, shrink)

    @pl.when(is_mid)
    def _():
        relay(1, 2)
        relay(3, 0)
        relay(1, 3)
        relay(3, 1)

    relation_of(0)

    @pl.when(is_mid)
    def _():
        relay(3, 2)

    @pl.when(is_end)
    def _():
        for k in pieces:
            arrived(2, k)

    relation_of(2)

    @pl.when(is_mid)
    def _():
        relay(3, 3)
        relation_of(1)

    result_beside = remote(to_end.at[0], deltas.at[2], dsend.at[4], drecv.at[2], beside)
    result_diagonal = remote(to_end.at[1], deltas.at[3], dsend.at[5], drecv.at[3], diagonal)

    @pl.when(is_mid)
    def _():
        rows_beside.wait_recv()
        rows_onward.wait_recv()
        shrink = None
        for k in range(CHUNKS):
            shrink = project(from_end.at[0], from_end.at[1], 0, pl.ds(k * step, step), shrink)
        delta = expand(shrink, 0)
        to_end[0] = delta[:2 * SLOTS]
        to_end[1] = delta[2 * SLOTS:]
        result_beside.start()
        result_diagonal.start()
        relation_of(3)

    @pl.when(is_end)
    def _():
        arrived(3, CHUNKS)
        relation_of(3, lambda k: arrived(3, k))
        result_beside.wait_recv()
        result_diagonal.wait_recv()

    @pl.when(is_mid)
    def _():
        delta_out(1).wait_recv()

    for q in (0, 2, 3):
        delta_out(q).wait_recv()

    for s in range(2):
        ordered = jnp.concatenate([deltas[g, s * SLOTS:(s + 1) * SLOTS, :] for g in range(8)], axis=0)
        high, low = halves(ordered)
        vsend[s] = base[s] + adapter_scale * (mm(unsort[...], high) + mm(unsort[...], low))
    value_out = remote(vsend, vrecv, vsem.at[0], vsem.at[1], peer)
    value_out.start()
    value_out.wait_recv()
    nv[...] = (vsend[...] + vrecv[...]).astype(jnp.bfloat16)

    def close(b, carry):
        at = pl.ds(pl.multiple_of(b * SLOTS, SLOTS), SLOTS)
        fresh_values = jnp.concatenate([nv[0, at, :], nv[1, at, :]], axis=0)
        result = ((ctx[b] + mm(wnew[b], fresh_values)) * inv[b]).astype(out.dtype)
        for s in range(2):
            for h in range(HQ):
                first = (s * HQ + h) * SLOTS
                out[s, at, h * HEAD_SIZE:(h + 1) * HEAD_SIZE] = result[first:first + SLOTS]
        return carry

    lax.fori_loop(0, blocks, close, 0)

    value_out.wait_send()
    cache_out.wait_send()
    own_out(CHUNKS).wait_send()
    for q in range(4):
        rows_across(q).wait_send()
    for q in (0, 2, 3):
        delta_out(q).wait_send()

    @pl.when(is_end)
    def _():
        rows_beside.wait_send()
        rows_onward.wait_send()

    @pl.when(is_mid)
    def _():
        for k in range(CHUNKS):
            own_out(k).wait_send()
        delta_out(1).wait_send()
        result_beside.wait_send()
        result_diagonal.wait_send()
        for slot in (1, 2, 3):
            for k in pieces:
                forward(slot, k).wait_send()


def fused_body(
    hidden,
    value_projection_weight,
    adapter_down_weight,
    adapter_up_weight,
    key_value_cache,
    query,
    fresh_token_keys,
    adapter_per_row,
    cache_length,
    adapter_storage_index,
):
    bf16, f32 = jnp.bfloat16, jnp.float32
    _, rows, width = hidden.shape
    rank = adapter_down_weight.shape[2]
    down = jnp.swapaxes(adapter_down_weight[0], 0, 1)
    blocks, tall = rows // SLOTS, 2 * HQ * SLOTS
    dma = pltpu.SemaphoreType.DMA
    return pl.pallas_call(
        fused_kernel,
        out_shape=jax.ShapeDtypeStruct(query.shape, bf16),
        in_specs=[pl.BlockSpec(memory_space=pltpu.HBM)] * 10,
        out_specs=pl.BlockSpec(memory_space=pltpu.VMEM),
        scratch_shapes=[
            pltpu.VMEM((1, rows), jnp.int32),
            pltpu.VMEM((1, rows), jnp.int32),
            pltpu.SMEM(adapter_storage_index.shape, jnp.int32),
            pltpu.VMEM(hidden.shape, bf16),
            pltpu.VMEM((width, HEAD_SIZE), bf16),
            pltpu.VMEM((4, rank, width), bf16),
            pltpu.VMEM((4, rank, HEAD_SIZE), bf16),
            pltpu.VMEM(query.shape, bf16),
            pltpu.VMEM((2,) + key_value_cache.shape, bf16),
            pltpu.VMEM(fresh_token_keys.shape, bf16),
            pltpu.VMEM((8, 2 * SLOTS, width), bf16),
            pltpu.VMEM((4, 2 * SLOTS, width), bf16),
            pltpu.VMEM((2, 2 * SLOTS, width), bf16),
            pltpu.VMEM((8, 2 * SLOTS, HEAD_SIZE), f32),
            pltpu.VMEM((4, 2 * SLOTS, HEAD_SIZE), f32),
            pltpu.VMEM((2, 2 * SLOTS, HEAD_SIZE), f32),
            pltpu.VMEM((2, rows, HEAD_SIZE), f32),
            pltpu.VMEM((2, rows, HEAD_SIZE), f32),
            pltpu.VMEM((2, rows, HEAD_SIZE), f32),
            pltpu.VMEM((blocks, tall, HEAD_SIZE), f32),
            pltpu.VMEM((blocks, tall, 2 * SLOTS), bf16),
            pltpu.VMEM((blocks, tall, 1), f32),
            pltpu.VMEM((rows, 1), jnp.int32),
            pltpu.VMEM((rows, rows), bf16),
            pltpu.VMEM((2, rows, HEAD_SIZE), bf16),
            dma((10,)),
            dma((4, CHUNKS + 1)),
            dma((4, CHUNKS + 1)),
            dma((2,)),
            dma((8,)),
            dma((4,)),
            dma((2,)),
            dma((6,)),
            dma((8,)),
            dma((2,)),
        ],
        compiler_params=pltpu.CompilerParams(
            collective_id=0, has_side_effects=True, vmem_limit_bytes=56 * 1024 * 1024
        ),
        cost_estimate=pl.CostEstimate(
            flops=2 * 4 * rows * width * HEAD_SIZE, bytes_accessed=6 << 20, transcendentals=rows * 2560
        ),
    )(
        hidden,
        value_projection_weight,
        down,
        adapter_up_weight[0],
        key_value_cache,
        query,
        fresh_token_keys,
        adapter_per_row.reshape(1, rows),
        cache_length.reshape(1, rows),
        adapter_storage_index,
    )


def solution(mesh):
    in_specs = (
        P(None, ("group", "batch"), "tensor"),
        P("tensor", None),
        P(("group", "batch"), "tensor", None),
        P(("group", "batch"), None, None),
        P(("group", "batch"), "tensor", None),
        P(None, ("group", "batch"), None),
        P(None, ("group", "batch"), None),
        P(("group", "batch"), None),
        P(("group", "batch")),
        P("group"),
    )
    out_specs = P(None, ("group", "batch"), None)
    small = mesh.shape["batch"] == 8 and mesh.shape["tensor"] == 2
    chosen = fused_body if small else body
    return jax.shard_map(chosen, mesh=mesh, in_specs=in_specs, out_specs=out_specs, check_vma=False)
```
